32 devices in a mesh: dev: 32 (over z, y, x, core).
Axes of the slice: x: 2, y: 2, z: 4, core: 2. Of those that a mesh axis runs over, the one named last changes fastest.
Arguments:
- samples: bfloat16 [1024, 201216], P('dev'), may hold values from -6 to 6
- input_gain: float32 [1024], P('dev'), may hold values from 0.3 to 4, as said below
Outputs:
- visibility: bfloat16 [768, 36, 2, 128, 128], P('dev')
The draws below stay inside these ranges and needn't reach their ends.
Inputs may be any that keep to these rules, and one draw needn't show every extreme that they name: `input_gain`: positive gains, one for each input.
All inputs are finite; a program needn't handle non-finite values.
Results may differ from the reference program's by a relative error of at most 0.0071.
Values may be sent and summed in bfloat16 or wider, within the bound.
A program may use at most 320 MiB of HBM per device.

```python
import math
import jax
import jax.numpy as jnp
import numpy as np
from jax import lax

INPUTS = 1024
FRAME = 1536
TAPS = 4
SPECTRA = 128
BLOCK = 128
CHANNELS = 768


def draw_input_gain(key, part):
    position = jnp.arange(INPUTS, dtype=jnp.int32).astype(jnp.float32) / max(INPUTS - 1, 1)
    rising = jnp.exp(0.5 * jnp.log(3.0) * position)
    spread = jnp.exp(jax.random.uniform(key, (INPUTS,), jnp.float32, jnp.log(0.7), jnp.log(1.4)))
    return (rising * spread).astype(jnp.float32)


def level_of(own_key, extent, shards, smallest, largest):
    loudness = 1.0
    for dim, parts in shards:
        steps = jax.random.uniform(jax.random.fold_in(jax.random.fold_in(own_key, 6), dim), (parts,), jnp.float32, smallest / len(shards), largest / len(shards))
        loudness = loudness * jnp.repeat(jnp.exp(steps), extent[dim] // parts).reshape((-1,) + (1,) * (len(extent) - 1 - dim))
    return loudness


def gaussian(own_key, extent, deviation, limit, cuts=(), kind=jnp.bfloat16):
    gain = level_of(own_key, extent, cuts, -0.22, 0.18) if cuts else 1.0
    drawn = jax.random.normal(own_key, extent, jnp.float32) * deviation * gain
    return jnp.minimum(jnp.maximum(drawn, -limit), limit).astype(kind)


def setup_inputs(seed: int = 0) -> dict:
    key_of = jax.random.split(jax.random.key(seed), 3)
    samples = gaussian(key_of[0], (INPUTS, (SPECTRA + TAPS - 1) * FRAME), 1.0, 6.0, ((0, 32),))
    input_gain = draw_input_gain(jax.random.fold_in(key_of[2], 71), 0)
    return dict(samples=samples, input_gain=input_gain)


def pfb_window():
    total = TAPS * FRAME
    position = jnp.arange(total, dtype=jnp.int32).astype(jnp.float32)
    centred = (position - total / 2 + 0.5) / FRAME
    taper = 0.54 - 0.46 * jnp.cos(2.0 * math.pi * position / (total - 1))
    return (jnp.sinc(centred) * taper).reshape(TAPS, FRAME)

def dft_table():
    sample_idx = jnp.arange(FRAME, dtype=jnp.int32)
    chan_idx = jnp.arange(CHANNELS, dtype=jnp.int32)
    phase = sample_idx[:, None] * chan_idx[None, :] % FRAME
    angle = 2.0 * math.pi / FRAME * phase.astype(jnp.float32)
    norm_factor = 1.0 / math.sqrt(FRAME)
    table = jnp.concatenate([jnp.cos(angle), -jnp.sin(angle)], axis=1) * norm_factor
    return table.astype(jnp.bfloat16)

def reference(samples, input_gain):
    window = pfb_window()
    table = dft_table()
    group = math.gcd(INPUTS, 64)
    frames = samples.reshape(INPUTS // group, group, SPECTRA + TAPS - 1, FRAME)
    gains = input_gain.reshape(INPUTS // group, group)

    def filter_group(args):
        block_frames, block_gain = args
        acc = jnp.zeros((group, SPECTRA, FRAME), jnp.float32)
        for tap in range(TAPS):
            acc = acc + window[tap][None, None, :] * block_frames[:, tap:tap + SPECTRA, :].astype(jnp.float32)
        filtered = acc.astype(jnp.bfloat16).reshape(group * SPECTRA, FRAME)
        spec = jnp.dot(filtered, table, preferred_element_type=jnp.float32)
        return spec.reshape(group, SPECTRA, 2 * CHANNELS) * block_gain[:, None, None]
    spectrum = lax.map(filter_group, (frames, gains)).reshape(INPUTS, SPECTRA, 2, CHANNELS)
    power = lax.optimization_barrier(jnp.sum(spectrum * spectrum, axis=(0, 1, 2)))
    level = 1.0 / jnp.sqrt(power / (INPUTS * SPECTRA) + 1e-06)
    quantized = (spectrum * level[None, None, None, :]).astype(jnp.bfloat16)
    per_channel = quantized.transpose(3, 0, 2, 1).reshape(CHANNELS, INPUTS, 2 * SPECTRA)
    nblk = INPUTS // BLOCK
    rows_np, cols_np = np.triu_indices(nblk)
    rows_idx = jnp.asarray(rows_np.astype(np.int32))
    cols_idx = jnp.asarray(cols_np.astype(np.int32))

    def one_channel(chan):
        tiles = chan.astype(jnp.float32).reshape(nblk, BLOCK, 2 * SPECTRA)
        left = jnp.take(tiles, rows_idx, axis=0)
        right = jnp.take(tiles, cols_idx, axis=0)
        turned = jnp.concatenate([-right[..., SPECTRA:], right[..., :SPECTRA]], axis=-1)
        real_part = jnp.einsum('pis,pjs->pij', left, right, precision=lax.Precision.HIGHEST)
        imag_part = jnp.einsum('pis,pjs->pij', left, turned, precision=lax.Precision.HIGHEST)
        stacked = jnp.stack([real_part, imag_part], axis=1) * (1.0 / SPECTRA)
        return stacked.astype(jnp.bfloat16)
    return lax.map(one_channel, per_channel)
```

```python
import functools
import math

import jax
import jax.numpy as jnp
import ml_dtypes
import numpy as np
from jax import lax
from jax.experimental import pallas as pl
from jax.experimental.pallas import tpu as pltpu
from jax.sharding import PartitionSpec as P

INPUTS = 1024
FRAME = 1536
TAPS = 4
BLOCK = 128
VMEM_LIMIT = 56 * 1024 * 1024


def pfb_window(frame_len, taps):
    total = taps * frame_len
    position = np.arange(total, dtype=np.float64)
    centred = (position - total / 2 + 0.5) / frame_len
    taper = 0.54 - 0.46 * np.cos(2.0 * math.pi * position / (total - 1))
    return (np.sinc(centred) * taper).reshape(taps, frame_len).astype(np.float32)


def dft_table(frame_len):
    channels = frame_len // 2
    phase = np.arange(channels)[:, None] * np.arange(frame_len)[None, :] % frame_len
    angle = 2.0 * math.pi / frame_len * phase
    table = np.stack([np.cos(angle), -np.sin(angle)]) / math.sqrt(frame_len)
    return table.astype(np.float32)


def chunk_sizes(count):
    if count % 6 == 0 and count >= 12:
        unit = count // 6
        return [unit, 2 * unit, 2 * unit, unit]
    return [1] * count if count <= 3 else [count // 2, count - count // 2]


def dft_kernel(group, spectra, gain_ref, table_ref, filt_ref, *refs):
    out_ref, turn_ref = refs[-2:]
    half = table_ref.shape[0] // 2
    first = pl.program_id(0) * group
    for pair in range(group // 2):
        rows = filt_ref[pl.ds(pair * 2 * spectra, 2 * spectra), :]
        spectrum = lax.dot_general(
            table_ref[...],
            rows,
            (((1,), (1,)), ((), ())),
            preferred_element_type=jnp.float32,
        )
        for sub in range(2):
            idx = pair * 2 + sub
            gain = gain_ref[first + idx]
            for part in range(2):
                piece = spectrum[
                    part * half : (part + 1) * half, sub * spectra : (sub + 1) * spectra
                ]
                turn_ref[part, pl.ds(idx, half, stride=group), :] = piece * gain
    for part in range(2):
        out_ref[:, :, part * spectra : (part + 1) * spectra] = (
            turn_ref[part].reshape(half, group, spectra).astype(out_ref.dtype)
        )


def dft(filtered, table, gain, local_inputs, spectra, earlier):
    rows, frame_len = table.shape
    half = rows // 2
    group = min(16, local_inputs)
    return pl.pallas_call(
        functools.partial(dft_kernel, group, spectra),
        grid=(local_inputs // group,),
        out_shape=jax.ShapeDtypeStruct((half, local_inputs, 2 * spectra), jnp.bfloat16),
        in_specs=[
            pl.BlockSpec(memory_space=pltpu.SMEM),
            pl.BlockSpec((rows, frame_len), lambda g: (0, 0)),
            pl.BlockSpec((group * spectra, frame_len), lambda g: (g, 0)),
        ]
        + [pl.BlockSpec(memory_space=pl.ANY)] * len(earlier),
        out_specs=pl.BlockSpec((half, group, 2 * spectra), lambda g: (0, g, 0)),
        scratch_shapes=[pltpu.VMEM((2, half * group, spectra), jnp.float32)],
        compiler_params=pltpu.CompilerParams(vmem_limit_bytes=VMEM_LIMIT),
        cost_estimate=pl.CostEstimate(
            flops=2 * rows * frame_len * local_inputs * spectra,
            bytes_accessed=2 * (rows * frame_len + local_inputs * spectra * (frame_len + rows)),
            transcendentals=0,
        ),
        name="dft",
    )(gain, table, filtered, *earlier)


def gram_kernel(samples_per_chan, spectra, *refs):
    recv_ref, out_ref = refs[0], refs[-1]
    num_dev, _, local_inputs, width = recv_ref.shape
    inputs = num_dev * local_inputs
    nblk = inputs // BLOCK
    chan = recv_ref[...].reshape(inputs, width)
    wide = chan.astype(jnp.float32)
    power = jnp.sum(wide * wide)
    scale = 1.0 / (power / samples_per_chan + 1e-06) / spectra
    turned = jnp.concatenate([-chan[:, spectra:], chan[:, :spectra]], axis=1)
    pair_of = {}
    for row in range(nblk):
        for col in range(row, nblk):
            pair_of[row, col] = len(pair_of)
    span = 2 if nblk % 2 == 0 else 1
    for col in range(0, nblk, span):
        left = chan[: (col + span) * BLOCK]
        for part, source in enumerate((chan, turned)):
            right = source[col * BLOCK : (col + span) * BLOCK]
            product = lax.dot_general(
                left, right, (((1,), (1,)), ((), ())), preferred_element_type=jnp.float32
            )
            product = (product * scale).astype(out_ref.dtype)
            for sub in range(span):
                for row in range(col + sub + 1):
                    out_ref[0, pair_of[row, col + sub], part] = product[
                        row * BLOCK : (row + 1) * BLOCK, sub * BLOCK : (sub + 1) * BLOCK
                    ]


def gram(received, earlier, start, total, spectra):
    num_dev, count, local_inputs, width = received.shape
    nblk = num_dev * local_inputs // BLOCK
    pairs = nblk * (nblk + 1) // 2
    out_shape = jax.ShapeDtypeStruct((total, pairs, 2, BLOCK, BLOCK), jnp.bfloat16)
    in_specs = [pl.BlockSpec((num_dev, 1, local_inputs, width), lambda k: (0, k, 0, 0))]
    args = [received]
    aliases = {}
    if earlier is not None:
        in_specs.append(pl.BlockSpec(memory_space=pl.ANY))
        args.append(earlier)
        aliases = {1: 0}
    return pl.pallas_call(
        functools.partial(gram_kernel, INPUTS * spectra, spectra),
        grid=(count,),
        out_shape=out_shape,
        in_specs=in_specs,
        out_specs=pl.BlockSpec((1, pairs, 2, BLOCK, BLOCK), lambda k: (start + k, 0, 0, 0, 0)),
        input_output_aliases=aliases,
        compiler_params=pltpu.CompilerParams(vmem_limit_bytes=VMEM_LIMIT),
        cost_estimate=pl.CostEstimate(
            flops=count * pairs * 4 * BLOCK * BLOCK * width,
            bytes_accessed=count * (pairs * 4 * BLOCK * BLOCK + 2 * width * num_dev * local_inputs),
            transcendentals=0,
        ),
        name="gram",
    )(*args)


def local(samples, input_gain):
    num_dev = lax.axis_size("dev")
    local_inputs = samples.shape[0]
    channels = FRAME // 2
    spectra = samples.shape[1] // FRAME - TAPS + 1
    local_chans = channels // num_dev
    window = jnp.asarray(pfb_window(FRAME, TAPS))
    table = dft_table(FRAME).reshape(2, num_dev, local_chans, FRAME)
    frames = samples.reshape(local_inputs, spectra + TAPS - 1, FRAME)
    acc = jnp.zeros((local_inputs, spectra, FRAME), jnp.float32)
    for tap in range(TAPS):
        acc = acc + window[tap][None, None, :] * frames[:, tap : tap + spectra, :].astype(
            jnp.float32
        )
    filtered = acc.astype(jnp.bfloat16).reshape(local_inputs * spectra, FRAME)
    visibility = None
    start = 0
    arrived = []
    before = []
    for count in chunk_sizes(local_chans):
        part = table[:, :, start : start + count].reshape(2 * num_dev * count, FRAME)
        part = jnp.asarray(part.astype(ml_dtypes.bfloat16))
        before = dft(filtered, part, input_gain, local_inputs, spectra, before)
        outgoing = before.reshape(num_dev, count, local_inputs, 2 * spectra)
        before = [before]
        received = lax.all_to_all(outgoing, "dev", split_axis=0, concat_axis=0, tiled=True)
        arrived.append((start, received))
        start += count
    for start, received in arrived:
        visibility = gram(received, visibility, start, local_chans, spectra)
    return visibility


def solution(mesh):
    in_specs = (P("dev", None), P("dev"))
    out_specs = P("dev", None, None, None, None)
    return jax.shard_map(local, mesh=mesh, in_specs=in_specs, out_specs=out_specs, check_vma=False)
```

```python
import functools
import math

import jax
import jax.numpy as jnp
import ml_dtypes
import numpy as np
from jax import lax
from jax.experimental import pallas as pl
from jax.experimental.pallas import tpu as pltpu
from jax.sharding import PartitionSpec as P

INPUTS = 1024
FRAME = 1536
TAPS = 4
BLOCK = 128
LANES = 128
VMEM_LIMIT = 56 * 1024 * 1024


def pfb_window(frame_len, taps):
    total = taps * frame_len
    position = np.arange(total, dtype=np.float64)
    centred = (position - total / 2 + 0.5) / frame_len
    taper = 0.54 - 0.46 * np.cos(2.0 * math.pi * position / (total - 1))
    return (np.sinc(centred) * taper).reshape(taps, frame_len).astype(np.float32)


def dft_table(frame_len):
    channels = frame_len // 2
    phase = np.arange(channels)[:, None] * np.arange(frame_len)[None, :] % frame_len
    angle = 2.0 * math.pi / frame_len * phase
    table = np.stack([np.cos(angle), -np.sin(angle)]) / math.sqrt(frame_len)
    return table.astype(np.float32)


def chunk_sizes(count):
    if count % 8 == 0:
        unit = count // 8
        return [unit, 6 * unit, unit]
    return [1] * count if count <= 3 else [count // 2, count - count // 2]


def filter_kernel(spectra, frame_len, samples_ref, window_ref, out_ref, turn_ref):
    group = samples_ref.shape[0]
    base = pl.program_id(1) * out_ref.shape[1]

    def columns(step, _):
        inside = pl.multiple_of(step * LANES, LANES)
        weights = [window_ref[tap : tap + 1, pl.ds(inside, LANES)] for tap in range(TAPS)]

        def frame(idx):
            at = pl.multiple_of(base + inside + idx * frame_len, LANES)
            return samples_ref[:, pl.ds(at, LANES)].astype(jnp.float32)

        held = [frame(idx) for idx in range(TAPS - 1)]
        for spectrum in range(spectra):
            held.append(frame(spectrum + TAPS - 1))
            acc = held[0] * weights[0]
            for tap in range(1, TAPS):
                acc = acc + held[tap] * weights[tap]
            turn_ref[step, pl.ds(spectrum, group, stride=spectra), :] = acc
            held.pop(0)
        return 0

    lax.fori_loop(0, turn_ref.shape[0], columns, 0)
    for step in range(turn_ref.shape[0]):
        out_ref[:, step * LANES : (step + 1) * LANES] = turn_ref[
            step, : group * spectra
        ].astype(out_ref.dtype)


def filterbank(samples, window, spectra):
    local_inputs, length = samples.shape
    frame_len = window.shape[1]
    group = min(16, local_inputs)
    width = frame_len // 3
    return pl.pallas_call(
        functools.partial(filter_kernel, spectra, frame_len),
        grid=(local_inputs // group, frame_len // width),
        out_shape=jax.ShapeDtypeStruct((local_inputs * spectra, frame_len), jnp.bfloat16),
        in_specs=[
            pl.BlockSpec((group, length), lambda g, j: (g, 0)),
            pl.BlockSpec((TAPS, width), lambda g, j: (0, j)),
        ],
        out_specs=pl.BlockSpec((group * spectra, width), lambda g, j: (g, j)),
        scratch_shapes=[pltpu.VMEM((width // LANES, (group + 1) * spectra, LANES), jnp.float32)],
        compiler_params=pltpu.CompilerParams(vmem_limit_bytes=VMEM_LIMIT),
        cost_estimate=pl.CostEstimate(
            flops=2 * TAPS * local_inputs * spectra * frame_len,
            bytes_accessed=2 * local_inputs * (length + spectra * frame_len),
            transcendentals=0,
        ),
        name="filterbank",
    )(samples, window)


def dft_kernel(group, spectra, gain_ref, table_ref, filt_ref, *refs):
    out_ref, turn_ref = refs[-2:]
    half = table_ref.shape[0] // 2
    first = pl.program_id(0) * group
    for pair in range(group // 2):
        rows = filt_ref[pl.ds(pair * 2 * spectra, 2 * spectra), :]
        spectrum = lax.dot_general(
            table_ref[...],
            rows,
            (((1,), (1,)), ((), ())),
            preferred_element_type=jnp.float32,
        )
        for sub in range(2):
            idx = pair * 2 + sub
            gain = gain_ref[first + idx]
            for part in range(2):
                piece = spectrum[
                    part * half : (part + 1) * half, sub * spectra : (sub + 1) * spectra
                ]
                turn_ref[part, pl.ds(idx, half, stride=group), :] = piece * gain
    for part in range(2):
        out_ref[:, :, part * spectra : (part + 1) * spectra] = (
            turn_ref[part, : half * group].reshape(half, group, spectra).astype(out_ref.dtype)
        )


def dft(filtered, table, gain, local_inputs, spectra, earlier):
    rows, frame_len = table.shape
    half = rows // 2
    group = min(16, local_inputs)
    return pl.pallas_call(
        functools.partial(dft_kernel, group, spectra),
        grid=(local_inputs // group,),
        out_shape=jax.ShapeDtypeStruct((half, local_inputs, 2 * spectra), jnp.bfloat16),
        in_specs=[
            pl.BlockSpec(memory_space=pltpu.SMEM),
            pl.BlockSpec((rows, frame_len), lambda g: (0, 0)),
            pl.BlockSpec((group * spectra, frame_len), lambda g: (g, 0)),
        ]
        + [pl.BlockSpec(memory_space=pl.ANY)] * len(earlier),
        out_specs=pl.BlockSpec((half, group, 2 * spectra), lambda g: (0, g, 0)),
        scratch_shapes=[pltpu.VMEM((2, (half + 1) * group, spectra), jnp.float32)],
        compiler_params=pltpu.CompilerParams(vmem_limit_bytes=VMEM_LIMIT),
        cost_estimate=pl.CostEstimate(
            flops=2 * rows * frame_len * local_inputs * spectra,
            bytes_accessed=2 * (rows * frame_len + local_inputs * spectra * (frame_len + rows)),
            transcendentals=0,
        ),
        name="dft",
    )(gain, table, filtered, *earlier)


def gram_kernel(samples_per_chan, spectra, *refs):
    recv_ref, out_ref = refs[0], refs[-1]
    num_dev, _, local_inputs, width = recv_ref.shape
    inputs = num_dev * local_inputs
    nblk = inputs // BLOCK
    chan = recv_ref[...].reshape(inputs, width)
    wide = chan.astype(jnp.float32)
    power = jnp.sum(wide * wide)
    scale = 1.0 / (power / samples_per_chan + 1e-06) / spectra
    turned = jnp.concatenate([-chan[:, spectra:], chan[:, :spectra]], axis=1)
    pair_of = {}
    for row in range(nblk):
        for col in range(row, nblk):
            pair_of[row, col] = len(pair_of)
    span = 2 if nblk % 2 == 0 else 1
    for col in range(0, nblk, span):
        left = chan[: (col + span) * BLOCK]
        for part, source in enumerate((chan, turned)):
            right = source[col * BLOCK : (col + span) * BLOCK]
            product = lax.dot_general(
                left, right, (((1,), (1,)), ((), ())), preferred_element_type=jnp.float32
            )
            product = (product * scale).astype(out_ref.dtype)
            for sub in range(span):
                for row in range(col + sub + 1):
                    out_ref[0, pair_of[row, col + sub], part] = product[
                        row * BLOCK : (row + 1) * BLOCK, sub * BLOCK : (sub + 1) * BLOCK
                    ]


def gram(received, earlier, start, total, spectra):
    num_dev, count, local_inputs, width = received.shape
    nblk = num_dev * local_inputs // BLOCK
    pairs = nblk * (nblk + 1) // 2
    out_shape = jax.ShapeDtypeStruct((total, pairs, 2, BLOCK, BLOCK), jnp.bfloat16)
    in_specs = [pl.BlockSpec((num_dev, 1, local_inputs, width), lambda k: (0, k, 0, 0))]
    args = [received]
    aliases = {}
    if earlier is not None:
        in_specs.append(pl.BlockSpec(memory_space=pl.ANY))
        args.append(earlier)
        aliases = {1: 0}
    return pl.pallas_call(
        functools.partial(gram_kernel, INPUTS * spectra, spectra),
        grid=(count,),
        out_shape=out_shape,
        in_specs=in_specs,
        out_specs=pl.BlockSpec((1, pairs, 2, BLOCK, BLOCK), lambda k: (start + k, 0, 0, 0, 0)),
        input_output_aliases=aliases,
        compiler_params=pltpu.CompilerParams(vmem_limit_bytes=VMEM_LIMIT),
        cost_estimate=pl.CostEstimate(
            flops=count * pairs * 4 * BLOCK * BLOCK * width,
            bytes_accessed=count * (pairs * 4 * BLOCK * BLOCK + 2 * width * num_dev * local_inputs),
            transcendentals=0,
        ),
        name="gram",
    )(*args)


def local(samples, input_gain):
    num_dev = lax.axis_size("dev")
    local_inputs = samples.shape[0]
    channels = FRAME // 2
    spectra = samples.shape[1] // FRAME - TAPS + 1
    local_chans = channels // num_dev
    window = jnp.asarray(pfb_window(FRAME, TAPS))
    table = dft_table(FRAME).reshape(2, num_dev, local_chans, FRAME)
    filtered = filterbank(samples, window, spectra)
    visibility = None
    start = 0
    arrived = []
    before = []
    for count in chunk_sizes(local_chans):
        part = table[:, :, start : start + count].reshape(2 * num_dev * count, FRAME)
        part = jnp.asarray(part.astype(ml_dtypes.bfloat16))
        before = dft(filtered, part, input_gain, local_inputs, spectra, before)
        outgoing = before.reshape(num_dev, count, local_inputs, 2 * spectra)
        before = [before]
        received = lax.all_to_all(outgoing, "dev", split_axis=0, concat_axis=0, tiled=True)
        arrived.append((start, received))
        start += count
    for start, received in arrived:
        visibility = gram(received, visibility, start, local_chans, spectra)
    return visibility


def solution(mesh):
    in_specs = (P("dev", None), P("dev"))
    out_specs = P("dev", None, None, None, None)
    return jax.shard_map(local, mesh=mesh, in_specs=in_specs, out_specs=out_specs, check_vma=False)
```
